512 devices in a mesh: head: 8 (over z_hi, x), ctx: 64 (over z_lo, y, core).
Axes of the slice: x: 4, y: 4, z: 16 (z_hi: 2, z_lo: 8; z = z_hi * 8 + z_lo), core: 2. Of those that a mesh axis runs over, the one named last changes fastest.
Arguments:
- queries: bfloat16 [128, 128, 8192], P('ctx', 'head'), may hold values from -4 to 4
- keys: bfloat16 [128, 128, 1024], P('ctx', 'head'), may hold values from -32 to 32
- values: bfloat16 [128, 128, 1024], P('ctx', 'head'), may hold values from -6 to 6
- doc_ids: int32 [128], replicated, may hold values from 0 to 15, never falling along the last dimension, each value on 1 to 65 neighbouring positions
Outputs:
- attended: bfloat16 [128, 128, 8192], P('ctx', 'head')
The draws below stay inside these ranges and needn't reach their ends.
Inputs may be any that keep to these rules, and one draw needn't show every extreme that they name: `doc_ids`: ids never fall along the blocks; every document covers 1 to 65 whole blocks, one of them exactly 65.
All inputs are finite; a program needn't handle non-finite values.
Results may differ from the reference program's by a relative error of at most 0.0045.
Values may be sent and summed in bfloat16 or wider, within the bound.
A program may use at most 64 MiB of HBM per device.

```python
import math
import jax
import jax.numpy as jnp
import numpy as np
from jax import lax

HD = 128
GROUP = 8
BLK = 128
KV_HEADS = 8
Q_HEADS = 64
BLOCKS = 128
MOST = 65
DOCS = 16


def query_base(key):
    shape = (BLOCKS, BLK, Q_HEADS * HD)
    normal_part = jnp.clip(jax.random.normal(key, shape, jnp.float32), -4.0, 4.0)
    return normal_part


def draw_queries(key, part):
    base = query_base(key)
    return base.astype(jnp.bfloat16)


def draw_keys(key, part):
    key = jax.random.fold_in(key, 2)
    shape = (BLOCKS, BLK, KV_HEADS * HD)
    own = jnp.clip(jax.random.normal(key, shape, jnp.float32), -4.0, 4.0)
    return own.astype(jnp.bfloat16)


def block_levels(stream_key, extent, pieces, smallest, high):
    gain = 1.0
    for axis_at, blocks in pieces:
        heights = jax.random.uniform(jax.random.fold_in(jax.random.fold_in(stream_key, 6), axis_at), (blocks,), jnp.float32, smallest / len(pieces), high / len(pieces))
        gain = gain * jnp.repeat(jnp.exp(heights), extent[axis_at] // blocks).reshape((-1,) + (1,) * (len(extent) - 1 - axis_at))
    return gain


def split_up(number_of, total, bound, lean):
    portions = [(1 << 20) // math.isqrt(grade ** lean) + 1 for grade in range(2, number_of + 1)]
    surplus, holding = total - bound - (number_of - 1), [1] * (number_of - 1)
    while surplus > 0:
        candidates = [i for i in range(number_of - 1) if holding[i] < bound]
        pool, remaining = sum([portions[i] for i in candidates]), surplus
        for i in candidates:
            addition = min(bound - holding[i], max(1, remaining * portions[i] // pool), surplus)
            holding[i] = holding[i] + addition
            surplus = surplus - addition
    return np.array([bound] + holding)


def uneven(rng, number_of, total, limit, slope):
    if number_of == 2:
        one = jax.random.randint(rng, (), max(1, total - limit), min(limit, total - 1) + 1)
        return jnp.stack([one, total - one])
    tallies = jnp.asarray(split_up(number_of, total, limit, slope), jnp.int32)
    twos = (number_of - 1) // 2
    giver, taker = tallies[1:1 + 2 * twos:2], tallies[2:2 + 2 * twos:2]
    margin = jnp.minimum(giver - 1, limit - taker)
    passed = jax.random.randint(jax.random.fold_in(rng, 1), (twos,), 0, 1 << 20) % (margin + 1)
    tallies = tallies.at[1:1 + 2 * twos:2].set(giver - passed).at[2:2 + 2 * twos:2].set(taker + passed)
    return tallies[jax.random.permutation(jax.random.fold_in(rng, 2), number_of)]


def centred(key, shape, width, reach, pieces=(), kind=jnp.bfloat16):
    values = width * jax.random.normal(key, shape, jnp.float32)
    if pieces:
        values = values * block_levels(key, shape, pieces, -0.22, 0.18)
    return jnp.clip(values, -reach, reach).astype(kind)


def setup_inputs(seed: int = 0) -> dict:
    key_of = jax.random.split(jax.random.key(seed), 5)
    queries = draw_queries(jax.random.fold_in(key_of[4], 71), 0)
    keys = draw_keys(jax.random.fold_in(key_of[4], 71), 0)
    values = centred(key_of[2], (BLOCKS, BLK, KV_HEADS * HD), 1.0, 6.0, ((0, 64), (1, 8)))
    doc_ids = jnp.searchsorted(jnp.cumsum(uneven(key_of[3], DOCS, BLOCKS, MOST, 2)), jnp.arange(BLOCKS), side="right").astype(jnp.int32)
    return dict(queries=queries, keys=keys, values=values, doc_ids=doc_ids)


def reference(queries, keys, values, doc_ids):
    total_tokens = BLOCKS * BLK
    query_blocks = queries.reshape(BLOCKS, BLK, KV_HEADS, GROUP, HD)
    key_rows = keys.reshape(total_tokens, KV_HEADS, HD).astype(jnp.float32)
    value_rows = values.reshape(total_tokens, KV_HEADS, HD).astype(jnp.float32)
    first_block = jnp.sum((doc_ids[None, :] < doc_ids[:, None]).astype(jnp.int32), axis=1).astype(jnp.int32)
    key_pos = jnp.arange(total_tokens, dtype=jnp.int32)
    scale = HD ** -0.5

    def one_block(packed):
        query_block, block_index, start_block = packed
        query_pos = block_index * BLK + jnp.arange(BLK, dtype=jnp.int32)
        allowed = (key_pos[None, :] <= query_pos[:, None]) & (key_pos[None, :] >= start_block * BLK)
        scores = jnp.einsum("qkgd,tkd->qkgt", query_block.astype(jnp.float32), key_rows) * scale
        allowed = allowed[:, None, None, :]
        rowmax = jnp.max(jnp.where(allowed, scores, -1e30), axis=-1)
        weights = jnp.where(allowed, jnp.exp(scores - rowmax[..., None]), 0.0)
        totals = jnp.sum(weights, axis=-1)
        rounded = lax.optimization_barrier(weights.astype(jnp.bfloat16)).astype(jnp.float32)
        mixed = jnp.einsum("qkgt,tkd->qkgd", rounded, value_rows) / totals[..., None]
        return mixed.reshape(BLK, KV_HEADS * GROUP * HD).astype(jnp.bfloat16)

    return lax.map(one_block, (query_blocks, jnp.arange(BLOCKS, dtype=jnp.int32), first_block))
```

```python
import jax
import jax.numpy as jnp
from jax import lax
from jax.experimental import pallas as pl
from jax.experimental.pallas import tpu as pltpu
from jax.sharding import PartitionSpec as P

HD = 128
GROUP = 8
BLK = 128
HALF = 64
COLS = GROUP * HD
NX, NZ, NLO = 4, 16, 8

BACK = (0, 1, 2, 3, 4, 4, 3, 2, 1, 0)
SLICES = len(BACK)
UP = {0: 1, 1: 2, 2: 3, 3: 5}
DOWN = {4: 6, 6: 7, 7: 8, 8: 9}
FAR = 4
KEYS = 16 * HALF
ROWS = GROUP * HALF
BIG = -1e30
SCALE = HD**-0.5 * 1.4426950408889634
MESH = pl.DeviceIdType.MESH

AT = {2: -1, 3: 4, 4: 6, 5: 8, 6: 10, 7: 14, 8: 18, 9: 22}
ACROSS = {1: 2, 2: 6, 3: 10, 4: 14, 5: 18, 6: 22, 7: 26, 8: 30, 9: 34}
TILES = 2


def kernel(
    doc_ref, q_ref, k_ref, v_ref, out_ref,
    kbuf, vbuf, q_in, qaug, kaug, vaug, acc, top, o_out,
    in_send, in_recv, hop_send, hop_recv, out_send, out_recv,
):
    head, ctx = lax.axis_index("head"), lax.axis_index("ctx")
    x, zhi = lax.rem(head, NX), lax.div(head, NX)
    lo, y, c = lax.div(ctx, 8), lax.rem(lax.div(ctx, 2), 4), lax.rem(ctx, 2)
    z = zhi * NLO + lo
    yh, ys = lax.div(y, 2), lax.rem(y, 2)

    def device(x, y, z, c):
        return (lax.div(z, NLO) * NX + x, lax.rem(z, NLO) * 8 + y * 2 + c)

    def turn(v, by, n):
        return lax.rem(v + by + n, n)

    def side(y):
        return lax.rem(lax.div(y + 1, 2), 2)

    y_pair = yh * 2 + 1 - ys
    y_same = 3 - y
    own, other = yh * 2 + c, (1 - yh) * 2 + c
    my_head = 2 * x + side(y)
    sibling = device(x, y, z, 1 - c)
    across = device(x, y_same, z, c)
    above = device(x, y, turn(z, 1, NZ), c)
    below = device(x, y, turn(z, -1, NZ), c)
    far_below = device(x, y, turn(z, -4, NZ), c)
    far_above = device(x, y, turn(z, 4, NZ), c)
    partners = [(dx, dy) for dx in range(NX) for dy in range(2)]

    barrier = pltpu.get_barrier_semaphore()
    greeted = [device(turn(x, dx, NX), (y, y_pair)[dy], z, c) for dx, dy in partners[1:]]
    greeted += [above, below, far_above, sibling, across]
    for one in greeted:
        pl.semaphore_signal(barrier, inc=1, device_id=one, device_id_type=MESH)
    pl.semaphore_wait(barrier, len(greeted))

    here = pl.ds(pl.multiple_of(x * 16, 16), 16)

    def inward(which, i):
        dx, dy = partners[i]
        xd, yd = turn(x, dx, NX), (y, y_pair)[dy]
        h = 2 * xd + side(yd)
        if which == 2:
            src = q_ref.at[:, :, pl.ds(pl.multiple_of(h * COLS, COLS), COLS)]
            dst = q_in.at[pl.ds(ys * 2, 2), here, :]
        else:
            src = (k_ref, v_ref)[which].at[:, :, pl.ds(pl.multiple_of(h * HD, HD), HD)]
            dst = (kbuf, vbuf)[which].at[0, own, pl.ds(ys * 2, 2), here, :]
        if i == 0:
            return pltpu.make_async_copy(src, dst, in_recv.at[which, 0])
        return pltpu.make_async_remote_copy(
            src_ref=src, dst_ref=dst, send_sem=in_send.at[which, i], recv_sem=in_recv.at[which, i],
            device_id=device(xd, yd, z, c), device_id_type=MESH,
        )

    def arrived(which):
        for i in range(len(partners)):
            copy = inward(which, i)
            copy.wait() if i == 0 else copy.wait_recv()

    for which in range(3):
        for i in range(len(partners)):
            inward(which, i).start()

    def hop(which, p, way):
        buf = (kbuf, vbuf)[which]
        src, dst_p, slot = own, p, 0
        if way == 0:
            dst_p, to = (UP[p], above) if p in UP else (DOWN[p], below)
        elif way == 1:
            to, slot = across, 1
        elif way == 2:
            to, slot = sibling, 2
        elif way == 3:
            src, to, slot = other, sibling, 3
        else:
            dst_p, to = FAR, far_below
        return pltpu.make_async_remote_copy(
            src_ref=buf.at[p, src], dst_ref=buf.at[dst_p, src],
            send_sem=hop_send.at[which, p, way], recv_sem=hop_recv.at[which, dst_p, slot],
            device_id=to, device_id_type=MESH,
        )

    def landed(which, p, slot):
        buf = (kbuf, vbuf)[which]
        pltpu.make_async_remote_copy(
            src_ref=buf.at[p, own], dst_ref=buf.at[p, own],
            send_sem=hop_send.at[which, p, 1], recv_sem=hop_recv.at[which, p, slot],
            device_id=across, device_id_type=MESH,
        ).wait_recv()

    def ways(p):
        return ([0] if p in UP or p in DOWN else []) + ([4] if p == 0 else []) + [1, 2]

    def forward(p):
        for which in range(2):
            if p == 0:
                arrived(which)
            else:
                landed(which, p, 0)
            for way in ways(p):
                hop(which, p, way).start()

    def cross(p):
        for which in range(2):
            landed(which, p, 1)
            hop(which, p, 3).start()

    def ready(p):
        for which in range(2):
            landed(which, p, 2)
            landed(which, p, 3)

    lane = lax.broadcasted_iota(jnp.int32, (1, HD), 1)
    row_of = lax.rem(lax.broadcasted_iota(jnp.int32, (ROWS, HD), 0), HALF)
    lanes = lax.broadcasted_iota(jnp.int32, (ROWS, HD), 1)
    for q in range(4):
        pick = (lanes == q) | (lanes == row_of + HALF)
        qaug[q, :, HD:] = jnp.where(pick, 1.0, 0.0).astype(jnp.bfloat16)
    vaug[:, HD:] = jnp.ones((KEYS, HD), jnp.bfloat16)
    for q in range(4):
        acc[q] = jnp.zeros((ROWS, 2 * HD), jnp.float32)
        top[q] = jnp.full((ROWS, HD), BIG, jnp.float32)

    forward(0)
    forward(1)
    cross(0)
    arrived(2)
    for q in range(4):
        for g in range(GROUP):
            qaug[q, pl.ds(g * HALF, HALF), :HD] = q_in[q, :, pl.ds(g * HD, HD)]
    for p, u in AT.items():
        if u < 0:
            forward(p)

    def prepare(p):
        kaug[:, :HD] = kbuf[p].reshape(KEYS, HD)
        vaug[:, :HD] = vbuf[p].reshape(KEYS, HD)
        back = jnp.int32(0)
        for at, by in enumerate(BACK):
            back = jnp.where(p == at, by, back)
        alike = (p == 0) | (zhi == 1)
        query_blocks = [lo * 16 + (yh * 2 + q // 2) * 4 + c * 2 + q % 2 for q in range(4)]
        query_docs = [doc_ref[b] for b in query_blocks]
        for i in range(16):
            block = (lo - back) * 16 + (i // 8 * 2 + i // 2 % 2) * 4 + i // 4 % 2 * 2 + i % 2
            doc = doc_ref[jnp.maximum(block, 0)]
            mask = jnp.zeros((1, HD), jnp.float32)
            for q in range(4):
                seen = (block < query_blocks[q]) | ((block == query_blocks[q]) & alike)
                seen = seen & (block >= 0) & (doc == query_docs[q])
                mask = jnp.where(lane == q, jnp.where(seen, 0.0, BIG), mask)
            kaug[pl.ds(i * HALF, HALF), HD:] = jnp.broadcast_to(mask, (HALF, HD)).astype(jnp.bfloat16)

    def triangle(q):
        tile_lane = lax.broadcasted_iota(jnp.int32, (HALF, HD), 1)
        tile_row = lax.broadcasted_iota(jnp.int32, (HALF, HD), 0)

        @pl.when(q > 0)
        def _():
            at = pl.ds(pl.multiple_of(own * 4 * HALF + (q - 1) * HALF, HALF), HALF)
            old = kaug[at, HD:].astype(jnp.float32)
            kaug[at, HD:] = jnp.where(tile_lane >= HALF, 0.0, old).astype(jnp.bfloat16)

        at = pl.ds(pl.multiple_of(own * 4 * HALF + q * HALF, HALF), HALF)
        old = kaug[at, HD:].astype(jnp.float32)
        hidden = tile_row > tile_lane - HALF
        new = jnp.where(tile_lane >= HALF, jnp.where(hidden, BIG, 0.0), old)
        kaug[at, HD:] = new.astype(jnp.bfloat16)

    def outward(dx, t):
        xd, yd = turn(x, dx, NX), yh * 2 + t
        src = o_out.at[pl.ds(t * 2, 2), pl.ds(pl.multiple_of(xd * 16, 16), 16), :]
        dst = out_ref.at[:, :, pl.ds(pl.multiple_of(my_head * COLS, COLS), COLS)]
        sem = out_recv.at[dx * 2 + ys]
        local = pltpu.make_async_copy(src, dst, sem)
        remote = pltpu.make_async_remote_copy(
            src_ref=src, dst_ref=dst, send_sem=out_send.at[dx * 2 + t], recv_sem=sem,
            device_id=device(xd, yd, z, c), device_id_type=MESH,
        )
        return local, remote

    def send_out(t):
        for dx in (2, 1, 3, 0):
            local, remote = outward(dx, t)
            if dx:
                remote.start()
            else:
                pl.when(ys == t)(local.start)
                pl.when(ys != t)(remote.start)

    events = {}
    for p in range(1, SLICES):
        if AT.get(p, -1) >= 0:
            events.setdefault(AT[p], []).append((forward, p))
        events.setdefault(ACROSS[p], []).append((cross, p))
    for p in range(SLICES):
        events.setdefault(p * 4, []).append((ready, p))
    events.setdefault(4 * SLICES - 2, []).append((send_out, 0))

    def unit(u, _):
        p, q = lax.div(u, 4), lax.rem(u, 4)
        for when, what in sorted(events.items()):

            @pl.when(u == when)
            def _(what=what):
                for act, arg in what:
                    act(arg)

        pl.when(q == 0)(lambda: prepare(p))
        pl.when(p == 0)(lambda: triangle(q))

        span = ROWS // TILES
        for r in range(TILES):
            rows = pl.ds(r * span, span)
            scores = lax.dot_general(
                qaug[q, rows, :], kaug[...], (((1,), (1,)), ((), ())), preferred_element_type=jnp.float32
            )
            before = top[q, rows, :]
            after = jnp.maximum(before, jnp.max(scores, axis=1, keepdims=True))
            weights = jnp.exp2((scores - jnp.concatenate([after] * (KEYS // HD), axis=1)) * SCALE)
            factor = jnp.exp2((before - after) * SCALE)
            mixed = jnp.dot(weights.astype(jnp.bfloat16), vaug[...], preferred_element_type=jnp.float32)
            acc[q, rows, :] = acc[q, rows, :] * jnp.concatenate([factor] * 2, axis=1) + mixed
            top[q, rows, :] = after

        @pl.when(p == SLICES - 1)
        def _():
            done = (acc[q, :, :HD] / acc[q, :, HD:]).astype(jnp.bfloat16)
            for g in range(GROUP):
                o_out[q, :, pl.ds(g * HD, HD)] = done[g * HALF : (g + 1) * HALF]

        return 0

    lax.fori_loop(0, 4 * SLICES, unit, 0)
    send_out(1)

    for i in range(1, len(partners)):
        for which in range(3):
            inward(which, i).wait_send()
    for p in range(SLICES):
        for which in range(2):
            for way in ways(p) + [3]:
                hop(which, p, way).wait_send()
    for t in range(2):
        for dx in range(NX):
            local, remote = outward(dx, t)
            if dx:
                remote.wait_send()
            else:
                pl.when(ys != t)(remote.wait_send)
    for dx in range(NX):
        for s in range(2):
            pltpu.make_async_copy(
                o_out.at[pl.ds(0, 2), pl.ds(0, 16), :],
                out_ref.at[:, :, pl.ds(0, COLS)],
                out_recv.at[dx * 2 + s],
            ).wait()


def on_device(queries, keys, values, doc_ids):
    bf16, f32 = jnp.bfloat16, jnp.float32
    anywhere = pl.BlockSpec(memory_space=pl.ANY)
    pieces = pltpu.VMEM((SLICES, 4, 4, HALF, HD), bf16)
    return pl.pallas_call(
        kernel,
        out_shape=jax.ShapeDtypeStruct(queries.shape, bf16),
        in_specs=[pl.BlockSpec(memory_space=pltpu.SMEM), anywhere, anywhere, anywhere],
        out_specs=anywhere,
        scratch_shapes=[
            pieces,
            pieces,
            pltpu.VMEM((4, HALF, COLS), bf16),
            pltpu.VMEM((4, ROWS, 2 * HD), bf16),
            pltpu.VMEM((KEYS, 2 * HD), bf16),
            pltpu.VMEM((KEYS, 2 * HD), bf16),
            pltpu.VMEM((4, ROWS, 2 * HD), f32),
            pltpu.VMEM((4, ROWS, HD), f32),
            pltpu.VMEM((4, HALF, COLS), bf16),
            pltpu.SemaphoreType.DMA((3, 8)),
            pltpu.SemaphoreType.DMA((3, 8)),
            pltpu.SemaphoreType.DMA((2, SLICES, 5)),
            pltpu.SemaphoreType.DMA((2, SLICES, 4)),
            pltpu.SemaphoreType.DMA((8,)),
            pltpu.SemaphoreType.DMA((8,)),
        ],
        compiler_params=pltpu.CompilerParams(
            collective_id=0, has_side_effects=True, vmem_limit_bytes=40 * 1024 * 1024
        ),
        cost_estimate=pl.CostEstimate(
            flops=4 * ROWS * 4 * KEYS * SLICES * HD, bytes_accessed=2 * queries.size * 2, transcendentals=0
        ),
    )(doc_ids, queries, keys, values)


def solution(mesh):
    in_specs = (P("ctx", "head", None), P("ctx", "head", None), P("ctx", "head", None), P())
    out_specs = P("ctx", "head", None)
    return jax.shard_map(
        on_device, mesh=mesh, in_specs=in_specs, out_specs=out_specs, check_vma=False
    )
```

```python
import jax
import jax.numpy as jnp
from jax import lax
from jax.experimental import pallas as pl
from jax.experimental.pallas import tpu as pltpu
from jax.sharding import PartitionSpec as P

HD = 128
GROUP = 8
BLK = 128
HALF = 64
COLS = GROUP * HD
NX, NZ, NLO = 4, 16, 8

BACK = (0, 1, 2, 3, 4, 4, 3, 2, 1, 0)
SLICES = len(BACK)
UP = {0: 1, 1: 2, 2: 3, 3: 5}
DOWN = {4: 6, 6: 7, 7: 8, 8: 9}
CROSS = ((1, 2, 3, 4, 5, 6, 7, 8), (0, 1, 2, 3, 6, 7, 8, 9))
UNITS = 9
HALF_KEYS = 8 * HALF
KEYS = 2 * HALF_KEYS
ROWS = GROUP * HALF
BIG = -1e30
SCALE = HD**-0.5 * 1.4426950408889634
MESH = pl.DeviceIdType.MESH
FAR_AT = {4: 1, 5: 3}
TRANSIT_AT, TURN_AT = 2, 6
FORWARD = {1: 2, 3: 3, 5: 4, 6: 5, 7: 6, 9: 7, 11: 8, 13: 9}


def kernel(
    doc_ref, q_ref, k_ref, v_ref, out_ref,
    kbuf, vbuf, transit, q_in, qaug, kaug, vaug, acc, top, o_out,
    in_send, in_recv, hop_send, hop_recv, transit_send, transit_recv, out_send, out_recv,
):
    head, ctx = lax.axis_index("head"), lax.axis_index("ctx")
    x, zhi = lax.rem(head, NX), lax.div(head, NX)
    lo, y, c = lax.div(ctx, 8), lax.rem(lax.div(ctx, 2), 4), lax.rem(ctx, 2)
    z = zhi * NLO + lo
    yh, ys = lax.div(y, 2), lax.rem(y, 2)

    def device(x, y, z, c):
        return (lax.div(z, NLO) * NX + x, lax.rem(z, NLO) * 8 + y * 2 + c)

    def turn(v, by, n):
        return lax.rem(v + by + n, n)

    def side(y):
        return lax.rem(lax.div(y + 1, 2), 2)

    y_pair = yh * 2 + 1 - ys
    y_same = 3 - y
    own, other = yh * 2 + c, (1 - yh) * 2 + c
    my_head = 2 * x + side(y)
    sibling = device(x, y, z, 1 - c)
    across = device(x, y_same, z, c)
    above = device(x, y, turn(z, 1, NZ), c)
    below = device(x, y, turn(z, -1, NZ), c)
    far_lo = jnp.minimum(lo + 4, NLO - 1)
    far = device(x, y, (1 - zhi) * NLO + far_lo, c)
    stop = device(x, y, (1 - zhi) * NLO + lax.rem(lo + 4, NLO), c)
    past_stop = device(x, y, zhi * NLO + lax.rem(lo + 4, NLO), c)
    rests, goes_up = (lo == 2) | (lo == 3), lo >= 6
    far_slot = jnp.where(lo < 4, 4, lo + 2)
    partners = [(dx, dy) for dx in range(NX) for dy in range(2)]
    to_above, to_below = lo < NLO - 1, lo > 0

    barrier = pltpu.get_barrier_semaphore()

    def greet(one):
        pl.semaphore_signal(barrier, inc=1, device_id=one, device_id_type=MESH)

    for dx, dy in partners[1:]:
        greet(device(turn(x, dx, NX), (y, y_pair)[dy], z, c))
    greet(sibling)
    greet(across)
    pl.when(to_above)(lambda: greet(above))
    pl.when(to_below)(lambda: greet(below))
    for source in range(6):
        pl.when(lo == min(source + 4, NLO - 1))(lambda: greet(device(x, y, (1 - zhi) * NLO + source, c)))
    pl.when(rests)(lambda: greet(stop))
    pl.when(goes_up)(lambda: greet(past_stop))
    count = to_above.astype(jnp.int32) + to_below.astype(jnp.int32) + rests.astype(jnp.int32)
    pl.semaphore_wait(barrier, 10 + count)

    here = pl.ds(pl.multiple_of(x * 16, 16), 16)

    def inward(which, i):
        dx, dy = partners[i]
        xd, yd = turn(x, dx, NX), (y, y_pair)[dy]
        h = 2 * xd + side(yd)
        if which == 2:
            src = q_ref.at[:, :, pl.ds(pl.multiple_of(h * COLS, COLS), COLS)]
            dst = q_in.at[pl.ds(ys * 2, 2), here, :]
        else:
            src = (k_ref, v_ref)[which].at[:, :, pl.ds(pl.multiple_of(h * HD, HD), HD)]
            dst = (kbuf, vbuf)[which].at[0, own, pl.ds(ys * 2, 2), here, :]
        if i == 0:
            return pltpu.make_async_copy(src, dst, in_recv.at[which, 0])
        return pltpu.make_async_remote_copy(
            src_ref=src, dst_ref=dst, send_sem=in_send.at[which, i], recv_sem=in_recv.at[which, i],
            device_id=device(xd, yd, z, c), device_id_type=MESH,
        )

    def arrived(which):
        for i in range(len(partners)):
            copy = inward(which, i)
            copy.wait() if i == 0 else copy.wait_recv()

    for which in range(3):
        for i in range(len(partners)):
            inward(which, i).start()

    def valid(p):
        back = jnp.int32(0)
        for at, by in enumerate(BACK):
            back = jnp.where(p == at, by, back)
        return lo >= back

    def hop(which, p, way):
        buf = (kbuf, vbuf)[which]
        src, dst_p, slot = own, p, 0
        if way == 0:
            dst_p, to = (UP[p], above) if p in UP else (DOWN[p], below) if p in DOWN else (8, above)
        elif way == 1:
            to, slot = across, 1
        elif way == 2:
            to, slot = sibling, 2
        elif way == 3:
            src, to, slot = other, sibling, 3
        else:
            dst_p, to = far_slot, far
        return pltpu.make_async_remote_copy(
            src_ref=buf.at[p, src], dst_ref=buf.at[dst_p, src],
            send_sem=hop_send.at[which, p, way], recv_sem=hop_recv.at[which, dst_p, slot],
            device_id=to, device_id_type=MESH,
        )

    def rest(which, leg):
        return pltpu.make_async_remote_copy(
            src_ref=transit.at[which] if leg else (kbuf, vbuf)[which].at[0, own],
            dst_ref=(kbuf, vbuf)[which].at[9, own] if leg else transit.at[which],
            send_sem=transit_send.at[which, leg],
            recv_sem=hop_recv.at[which, 9, 0] if leg else transit_recv.at[which],
            device_id=past_stop if leg else stop, device_id_type=MESH,
        )

    def landed(which, p, slot):
        buf = (kbuf, vbuf)[which]
        pltpu.make_async_remote_copy(
            src_ref=buf.at[p, own], dst_ref=buf.at[p, own],
            send_sem=hop_send.at[which, p, 1], recv_sem=hop_recv.at[which, p, slot],
            device_id=across, device_id_type=MESH,
        ).wait_recv()

    def sends(which, p, act, early=True):
        if p in UP:
            pl.when(to_above)(lambda: act(hop(which, p, 0)))
        elif p == 8:
            pl.when(lo < NLO - 1)(lambda: act(hop(which, p, 0)))
        elif p in DOWN:
            act(hop(which, p, 0))
        if p == 0 and early:
            pl.when(lo < 4)(lambda: act(hop(which, p, 4)))
            pl.when(goes_up)(lambda: act(rest(which, 0)))
        if p in (4, 5):
            pl.when(yh == 1)(lambda: act(hop(which, p, 1)))
        elif p in (0, 9):
            pl.when(yh == 0)(lambda: act(hop(which, p, 1)))
        else:
            act(hop(which, p, 1))
        act(hop(which, p, 2))

    def forward(p):
        @pl.when(valid(p))
        def _():
            for which in range(2):
                if p == 0:
                    arrived(which)
                elif p == 9:
                    pl.when(lo != 6)(lambda: landed(which, p, 0))
                else:
                    landed(which, p, 0)
                sends(which, p, lambda copy: copy.start())

    def crossed(m):
        p = jnp.int32(0)
        for at in range(len(CROSS[0])):
            p = jnp.where(m == at, jnp.where(yh == 0, CROSS[0][at], CROSS[1][at]), p)
        return p

    def cross(m):
        p = crossed(m)

        @pl.when(valid(p))
        def _():
            for which in range(2):
                landed(which, p, 1)
                hop(which, p, 3).start()

    def ready(p, slot):
        @pl.when(valid(p))
        def _():
            for which in range(2):
                landed(which, p, slot)

    lane = lax.broadcasted_iota(jnp.int32, (1, HD), 1)
    lanes = lax.broadcasted_iota(jnp.int32, (ROWS, HD), 1)
    ones = jnp.ones((HALF, HD), jnp.bfloat16)
    for q in range(4):
        qaug[q, :, HD:] = jnp.where(lanes == q, 1.0, 0.0).astype(jnp.bfloat16)
    vaug[:, HD:] = jnp.ones((KEYS, HD), jnp.bfloat16)

    forward(0)
    forward(1)
    arrived(2)
    for q in range(4):
        for g in range(GROUP):
            qaug[q, pl.ds(g * HALF, HALF), :HD] = q_in[q, :, pl.ds(g * HD, HD)]

    for q in range(4):
        block_keys = kbuf[0, own, q]
        block_values = jnp.concatenate([vbuf[0, own, q], ones], axis=1)
        scores = lax.dot_general(
            qaug[q, :, :HD], block_keys, (((1,), (1,)), ((), ())), preferred_element_type=jnp.float32
        )
        key = lax.broadcasted_iota(jnp.int32, (ROWS, HALF), 1)
        token = lax.rem(lax.broadcasted_iota(jnp.int32, (ROWS, HALF), 0), HALF)
        scores = jnp.where(key <= token, scores, BIG)
        best = jnp.max(scores, axis=1, keepdims=True)
        weights = jnp.exp2((scores - best) * SCALE)
        acc[q] = jnp.dot(weights.astype(jnp.bfloat16), block_values, preferred_element_type=jnp.float32)
        top[q] = jnp.broadcast_to(best, (ROWS, HD))

    query_blocks = [lo * 16 + (yh * 2 + q // 2) * 4 + c * 2 + q % 2 for q in range(4)]

    def prepare(p, half_of_y, at):
        there = valid(p)
        rows = pl.ds(at * HALF_KEYS, HALF_KEYS)

        @pl.when(there)
        def _():
            kaug[rows, :HD] = kbuf[p, pl.ds(half_of_y * 2, 2)].reshape(HALF_KEYS, HD)
            vaug[rows, :HD] = vbuf[p, pl.ds(half_of_y * 2, 2)].reshape(HALF_KEYS, HD)

        @pl.when(jnp.logical_not(there))
        def _():
            kaug[rows, :HD] = jnp.zeros((HALF_KEYS, HD), jnp.bfloat16)
            vaug[rows, :HD] = jnp.zeros((HALF_KEYS, HD), jnp.bfloat16)

        back = jnp.int32(0)
        for slot, by in enumerate(BACK):
            back = jnp.where(p == slot, by, back)
        alike = (p != 0) & (zhi == 1)
        docs = [doc_ref[b] for b in query_blocks]
        for i in range(8):
            block = (lo - back) * 16 + (half_of_y * 2 + i // 2 % 2) * 4 + i // 4 * 2 + i % 2
            doc = doc_ref[jnp.maximum(block, 0)]
            mask = jnp.zeros((1, HD), jnp.float32)
            for q in range(4):
                seen = (block < query_blocks[q]) | ((block == query_blocks[q]) & alike)
                seen = seen & (block >= 0) & (doc == docs[q])
                mask = jnp.where(lane == q, jnp.where(seen, 0.0, BIG), mask)
            tile = pl.ds(at * HALF_KEYS + i * HALF, HALF)
            kaug[tile, HD:] = jnp.broadcast_to(mask, (HALF, HD)).astype(jnp.bfloat16)

    def outward(dx, t):
        xd, yd = turn(x, dx, NX), yh * 2 + t
        src = o_out.at[pl.ds(t * 2, 2), pl.ds(pl.multiple_of(xd * 16, 16), 16), :]
        dst = out_ref.at[:, :, pl.ds(pl.multiple_of(my_head * COLS, COLS), COLS)]
        sem = out_recv.at[dx * 2 + ys]
        local = pltpu.make_async_copy(src, dst, sem)
        remote = pltpu.make_async_remote_copy(
            src_ref=src, dst_ref=dst, send_sem=out_send.at[dx * 2 + t], recv_sem=sem,
            device_id=device(xd, yd, z, c), device_id_type=MESH,
        )
        return local, remote

    def send_out(t):
        for dx in (2, 1, 3, 0):
            local, remote = outward(dx, t)
            if dx:
                remote.start()
            else:
                pl.when(ys == t)(local.start)
                pl.when(ys != t)(remote.start)

    def send_far(source):
        @pl.when(lo == source)
        def _():
            for which in range(2):
                hop(which, 0, 4).start()

    def pass_on():
        @pl.when(rests)
        def _():
            for which in range(2):
                rest(which, 0).wait_recv()
                rest(which, 1).start()

    def turn_up():
        @pl.when(lo == 6)
        def _():
            for which in range(2):
                landed(which, 9, 0)
                hop(which, 9, 0).start()

    events = {TRANSIT_AT: [pass_on], TURN_AT: [turn_up]}
    for source, u in FAR_AT.items():
        events.setdefault(u, []).append(lambda source=source: send_far(source))
    for u, p in FORWARD.items():
        events.setdefault(u, []).append(lambda p=p: forward(p))
    for m in range(len(CROSS[0])):
        events.setdefault(2 * m + 1, []).append(lambda m=m: cross(m))
        events.setdefault(2 * m + 2, []).append(lambda m=m: ready(crossed(m), 3))
    for p in range(SLICES):
        events.setdefault(max(0, 2 * (p - 1)), []).append(lambda p=p: ready(p, 2))
    events.setdefault(2 * UNITS - 1, []).append(lambda: send_out(0))

    def half_unit(u, _):
        i, h = lax.div(u, 2), lax.rem(u, 2)
        for when, what in sorted(events.items()):

            @pl.when(u == when)
            def _(what=what):
                for act in what:
                    act()

        first = jnp.where(i == 0, 0, crossed(i - 1))
        second = i + 1

        @pl.when(valid(first) | valid(second))
        def _():
            @pl.when(h == 0)
            def _():
                prepare(first, jnp.where(i == 0, yh, 1 - yh), 0)
                prepare(second, yh, 1)

            def scores_of(q):
                return lax.dot_general(
                    qaug[q], kaug[...], (((1,), (1,)), ((), ())), preferred_element_type=jnp.float32
                )

            def soften(q, scores):
                before = top[q]
                after = jnp.maximum(before, jnp.max(scores, axis=1, keepdims=True))
                top[q] = after
                weights = jnp.exp2((scores - jnp.concatenate([after] * (KEYS // HD), axis=1)) * SCALE)
                return weights.astype(jnp.bfloat16), jnp.exp2((before - after) * SCALE)

            def mix(q, weights, factor):
                mixed = jnp.dot(weights, vaug[...], preferred_element_type=jnp.float32)
                acc[q] = acc[q] * jnp.concatenate([factor] * 2, axis=1) + mixed

            q = h * 2
            scores = scores_of(q)
            later_scores = scores_of(q + 1)
            weights, factor = soften(q, scores)
            later = soften(q + 1, later_scores)
            mix(q, weights, factor)
            mix(q + 1, *later)

        @pl.when(i == UNITS - 1)
        def _():
            for j in range(2):
                q = h * 2 + j
                done = (acc[q, :, :HD] / acc[q, :, HD:]).astype(jnp.bfloat16)
                for g in range(GROUP):
                    o_out[q, :, pl.ds(g * HD, HD)] = done[g * HALF : (g + 1) * HALF]

        return 0

    lax.fori_loop(0, 2 * UNITS, half_unit, 0)
    send_out(1)

    for i in range(1, len(partners)):
        for which in range(3):
            inward(which, i).wait_send()
    for p in range(SLICES):

        @pl.when(valid(p))
        def _(p=p):
            for which in range(2):
                sends(which, p, lambda copy: copy.wait_send(), False)
                if p == 0:
                    pl.when(lo < 6)(lambda: hop(which, 0, 4).wait_send())
                    pl.when(goes_up)(lambda: rest(which, 0).wait_send())
                if p == 9:
                    pl.when(rests)(lambda: rest(which, 1).wait_send())
                    pl.when(lo == 6)(lambda: hop(which, 9, 0).wait_send())

    for m in range(len(CROSS[0])):
        p = crossed(m)

        @pl.when(valid(p))
        def _(p=p):
            for which in range(2):
                hop(which, p, 3).wait_send()

    for t in range(2):
        for dx in range(NX):
            local, remote = outward(dx, t)
            if dx:
                remote.wait_send()
            else:
                pl.when(ys != t)(remote.wait_send)
    for dx in range(NX):
        for s in range(2):
            pltpu.make_async_copy(
                o_out.at[pl.ds(0, 2), pl.ds(0, 16), :],
                out_ref.at[:, :, pl.ds(0, COLS)],
                out_recv.at[dx * 2 + s],
            ).wait()


def on_device(queries, keys, values, doc_ids):
    bf16, f32 = jnp.bfloat16, jnp.float32
    anywhere = pl.BlockSpec(memory_space=pl.ANY)
    pieces = pltpu.VMEM((SLICES, 4, 4, HALF, HD), bf16)
    return pl.pallas_call(
        kernel,
        out_shape=jax.ShapeDtypeStruct(queries.shape, bf16),
        in_specs=[pl.BlockSpec(memory_space=pltpu.SMEM)] + [pl.BlockSpec(memory_space=pltpu.HBM)] * 3,
        out_specs=anywhere,
        scratch_shapes=[
            pieces,
            pieces,
            pltpu.VMEM((2, 4, HALF, HD), bf16),
            pltpu.VMEM((4, HALF, COLS), bf16),
            pltpu.VMEM((4, ROWS, 2 * HD), bf16),
            pltpu.VMEM((KEYS, 2 * HD), bf16),
            pltpu.VMEM((KEYS, 2 * HD), bf16),
            pltpu.VMEM((4, ROWS, 2 * HD), f32),
            pltpu.VMEM((4, ROWS, HD), f32),
            pltpu.VMEM((4, HALF, COLS), bf16),
            pltpu.SemaphoreType.DMA((3, 8)),
            pltpu.SemaphoreType.DMA((3, 8)),
            pltpu.SemaphoreType.DMA((2, SLICES, 5)),
            pltpu.SemaphoreType.DMA((2, SLICES, 4)),
            pltpu.SemaphoreType.DMA((2, 2)),
            pltpu.SemaphoreType.DMA((2,)),
            pltpu.SemaphoreType.DMA((8,)),
            pltpu.SemaphoreType.DMA((8,)),
        ],
        compiler_params=pltpu.CompilerParams(
            collective_id=0, has_side_effects=True, vmem_limit_bytes=62 * 1024 * 1024
        ),
        cost_estimate=pl.CostEstimate(
            flops=4 * ROWS * 4 * KEYS * UNITS * HD, bytes_accessed=2 * queries.size * 2, transcendentals=0
        ),
    )(doc_ids, queries, keys, values)


def solution(mesh):
    in_specs = (P("ctx", "head", None), P("ctx", "head", None), P("ctx", "head", None), P())
    out_specs = P("ctx", "head", None)
    return jax.shard_map(
        on_device, mesh=mesh, in_specs=in_specs, out_specs=out_specs, check_vma=False
    )
```

```python
import jax
import jax.numpy as jnp
from jax import lax
from jax.experimental import pallas as pl
from jax.experimental.pallas import tpu as pltpu
from jax.sharding import PartitionSpec as P

HD = 128
GROUP = 8
BLK = 128
HALF = 64
COLS = GROUP * HD
NX, NZ, NLO = 4, 16, 8

SLICES = 10
UNITS = 9
HALF_KEYS = 8 * HALF
KEYS = 2 * HALF_KEYS
ROWS = GROUP * HALF
BIG = -1e30
SCALE = HD**-0.5 * 1.4426950408889634
MESH = pl.DeviceIdType.MESH
FAR_AT = {4: 1, 5: 2}
TRANSIT_AT, TURN_AT = 5, 8


def back_of(p):
    return jnp.minimum(jnp.minimum(p, 4), SLICES - 1 - p)


def onward_of(p):
    return p + 1 + ((p == 3) | (p == 4)).astype(jnp.int32)


def kernel(
    doc_ref, q_ref, k_ref, v_ref, out_ref,
    kv, transit, q_in, qaug, kaug, vaug, acc, top, o_out,
    in_send, in_recv, hop_send, hop_recv, transit_send, transit_recv, out_send, out_recv, ack,
):
    head, ctx = lax.axis_index("head"), lax.axis_index("ctx")
    x, zhi = lax.rem(head, NX), lax.div(head, NX)
    lo, y, c = lax.div(ctx, 8), lax.rem(lax.div(ctx, 2), 4), lax.rem(ctx, 2)
    z = zhi * NLO + lo
    yh, ys = lax.div(y, 2), lax.rem(y, 2)

    def device(x, y, z, c):
        return (lax.div(z, NLO) * NX + x, lax.rem(z, NLO) * 8 + y * 2 + c)

    def turn(v, by, n):
        return lax.rem(v + by + n, n)

    def side(y):
        return lax.rem(lax.div(y + 1, 2), 2)

    y_pair = yh * 2 + 1 - ys
    y_same = 3 - y
    own, other = yh * 2 + c, (1 - yh) * 2 + c
    my_head = 2 * x + side(y)
    sibling = device(x, y, z, 1 - c)
    across = device(x, y_same, z, c)
    above = device(x, y, turn(z, 1, NZ), c)
    below = device(x, y, turn(z, -1, NZ), c)
    far_lo = jnp.minimum(lo + 4, NLO - 1)
    far = device(x, y, (1 - zhi) * NLO + far_lo, c)
    stop = device(x, y, (1 - zhi) * NLO + lax.rem(lo + 4, NLO), c)
    past_stop = device(x, y, zhi * NLO + lax.rem(lo + 4, NLO), c)
    rests, goes_up = (lo == 2) | (lo == 3), lo >= 6
    far_slot = jnp.where(lo < 4, 4, lo + 2)
    partners = [(dx, dy) for dx in range(NX) for dy in range(2)]
    to_above, to_below = lo < NLO - 1, lo > 0

    barrier = pltpu.get_barrier_semaphore()

    def greet(one):
        pl.semaphore_signal(barrier, inc=1, device_id=one, device_id_type=MESH)

    for dx, dy in partners[1:]:
        greet(device(turn(x, dx, NX), (y, y_pair)[dy], z, c))
    greet(sibling)
    greet(across)
    pl.when(to_above)(lambda: greet(above))
    pl.when(to_below)(lambda: greet(below))
    pl.when(goes_up)(lambda: greet(past_stop))

    def from_other_half(tell):
        for source in range(6):
            pl.when(lo == min(source + 4, NLO - 1))(lambda: tell(device(x, y, (1 - zhi) * NLO + source, c)))
        pl.when(rests)(lambda: tell(stop))

    pl.when(zhi == 0)(lambda: from_other_half(greet))
    pl.when((zhi == 0) & (lo < 6))(lambda: greet(far))
    pl.when((zhi == 0) & goes_up)(lambda: greet(stop))
    welcomed = jnp.where(lo == NLO - 1, 3, jnp.where(lo >= 2, 1, 0))
    count = to_above.astype(jnp.int32) + to_below.astype(jnp.int32) + rests.astype(jnp.int32)
    pl.semaphore_wait(barrier, 9 + zhi * (1 + welcomed) + count)

    def welcome(one):
        pl.semaphore_signal(ack, inc=1, device_id=one, device_id_type=MESH)

    pl.when(zhi == 1)(lambda: from_other_half(welcome))

    here = pl.ds(pl.multiple_of(x * 16, 16), 16)

    def inward(which, i):
        xd, yd = turn(x, lax.div(i, 2), NX), jnp.where(lax.rem(i, 2) == 0, y, y_pair)
        h = 2 * xd + side(yd)
        if which == 2:
            src = q_ref.at[:, :, pl.ds(pl.multiple_of(h * COLS, COLS), COLS)]
            dst = q_in.at[pl.ds(ys * 2, 2), here, :]
        else:
            src = (k_ref, v_ref)[which].at[:, :, pl.ds(pl.multiple_of(h * HD, HD), HD)]
            dst = kv.at[which, 0, own, pl.ds(ys * 2, 2), here, :]
        local = pltpu.make_async_copy(src, dst, in_recv.at[which, 0])
        remote = pltpu.make_async_remote_copy(
            src_ref=src, dst_ref=dst, send_sem=in_send.at[which, i], recv_sem=in_recv.at[which, i],
            device_id=device(xd, yd, z, c), device_id_type=MESH,
        )
        return local, remote

    def each(first, last, act):
        def step(i, _):
            act(i)
            return 0

        lax.fori_loop(first, last, step, 0)

    def arrived(which):
        inward(which, jnp.int32(0))[0].wait()
        each(1, 2 * NX, lambda i: inward(which, i)[1].wait_recv())

    for which in range(3):
        inward(which, jnp.int32(0))[0].start()
        each(1, 2 * NX, lambda i: inward(which, i)[1].start())

    def valid(p):
        return lo >= back_of(p)

    def hop(which, p, way):
        src, dst_p, slot = own, p, 0
        if way == 0:
            dst_p, to = onward_of(p), device(x, y, turn(z, jnp.where(p < 4, 1, -1), NZ), c)
        elif way == 1:
            to, slot = across, 1
        elif way == 2:
            to, slot = sibling, 2
        elif way == 3:
            src, to, slot = other, sibling, 3
        elif way == 4:
            dst_p, to = far_slot, far
        else:
            dst_p, to = 8, above
        return pltpu.make_async_remote_copy(
            src_ref=kv.at[which, p, src], dst_ref=kv.at[which, dst_p, src],
            send_sem=hop_send.at[which, p, way], recv_sem=hop_recv.at[which, dst_p, slot],
            device_id=to, device_id_type=MESH,
        )

    def rest(which, leg):
        return pltpu.make_async_remote_copy(
            src_ref=transit.at[which] if leg else kv.at[which, 0, own],
            dst_ref=kv.at[which, 9, own] if leg else transit.at[which],
            send_sem=transit_send.at[which, leg],
            recv_sem=hop_recv.at[which, 9, 0] if leg else transit_recv.at[which],
            device_id=past_stop if leg else stop, device_id_type=MESH,
        )

    def landed(which, p, slot):
        pltpu.make_async_remote_copy(
            src_ref=kv.at[which, p, own], dst_ref=kv.at[which, p, own],
            send_sem=hop_send.at[which, p, 1], recv_sem=hop_recv.at[which, p, slot],
            device_id=across, device_id_type=MESH,
        ).wait_recv()

    def sends(which, p, act):
        up, down = (p < 4) & to_above, (p == 4) | (p == 6) | (p == 7) | ((p == 8) & (lo < NLO - 1))
        pl.when(up | down)(lambda: act(hop(which, p, 0)))
        to_upper, to_lower = (p != 4) & (p != 5), (p != 0) & (p != 9)
        pl.when(((yh == 0) & to_upper) | ((yh == 1) & to_lower))(lambda: act(hop(which, p, 1)))
        act(hop(which, p, 2))

    def forward(which, p):
        @pl.when(valid(p))
        def _():
            pl.when((p != 9) | (lo != 6))(lambda: landed(which, p, 0))
            sends(which, p, lambda copy: copy.start())

    def crossed(m):
        return jnp.where(yh == 0, m + 1, jnp.where(m < 4, m, m + 2))

    def cross(which, m):
        p = crossed(m)

        @pl.when(valid(p))
        def _():
            landed(which, p, 1)
            hop(which, p, 3).start()

    def ready(p, slot):
        @pl.when(valid(p))
        def _():
            for which in range(2):
                landed(which, p, slot)

    lane = lax.broadcasted_iota(jnp.int32, (1, HD), 1)
    lanes = lax.broadcasted_iota(jnp.int32, (ROWS, HD), 1)
    ones = jnp.ones((HALF, HD), jnp.bfloat16)

    def mark(q):
        qaug[q, :, HD:] = jnp.where(lanes == q, 1.0, 0.0).astype(jnp.bfloat16)

    each(0, 4, mark)

    def fill(i):
        vaug[pl.ds(pl.multiple_of(i * HALF, HALF), HALF), HD:] = ones

    each(0, KEYS // HALF, fill)

    for which in range(2):
        arrived(which)
        sends(which, jnp.int32(0), lambda copy: copy.start())
        pl.when((zhi == 1) & (lo < 4))(lambda: hop(which, 0, 4).start())
        pl.when((zhi == 1) & goes_up)(lambda: rest(which, 0).start())
    each(0, 2, lambda which: forward(which, jnp.int32(1)))
    arrived(2)

    def begin(q):
        for g in range(GROUP):
            qaug[q, pl.ds(g * HALF, HALF), :HD] = q_in[q, :, pl.ds(g * HD, HD)]
        block_values = jnp.concatenate([kv[1, 0, own, q], ones], axis=1)
        scores = lax.dot_general(
            qaug[q, :, :HD], kv[0, 0, own, q], (((1,), (1,)), ((), ())), preferred_element_type=jnp.float32
        )
        key = lax.broadcasted_iota(jnp.int32, (ROWS, HALF), 1)
        token = lax.rem(lax.broadcasted_iota(jnp.int32, (ROWS, HALF), 0), HALF)
        scores = jnp.where(key <= token, scores, BIG)
        best = jnp.max(scores, axis=1, keepdims=True)
        weights = jnp.exp2((scores - best) * SCALE)
        acc[q] = jnp.dot(weights.astype(jnp.bfloat16), block_values, preferred_element_type=jnp.float32)
        top[q] = jnp.broadcast_to(best, (ROWS, HD))

    each(0, 4, begin)

    query_blocks = [lo * 16 + (yh * 2 + q // 2) * 4 + c * 2 + q % 2 for q in range(4)]

    def prepare(p, half_of_y, at):
        there = valid(p)
        rows = pl.ds(pl.multiple_of(at * HALF_KEYS, HALF_KEYS), HALF_KEYS)

        @pl.when(there)
        def _():
            kaug[rows, :HD] = kv[0, p, pl.ds(half_of_y * 2, 2)].reshape(HALF_KEYS, HD)
            vaug[rows, :HD] = kv[1, p, pl.ds(half_of_y * 2, 2)].reshape(HALF_KEYS, HD)

        @pl.when(jnp.logical_not(there))
        def _():
            kaug[rows, :HD] = jnp.zeros((HALF_KEYS, HD), jnp.bfloat16)
            vaug[rows, :HD] = jnp.zeros((HALF_KEYS, HD), jnp.bfloat16)

        back = back_of(p)
        alike = (p != 0) & (zhi == 1)
        docs = [doc_ref[b] for b in query_blocks]
        for i in range(8):
            block = (lo - back) * 16 + (half_of_y * 2 + i // 2 % 2) * 4 + i // 4 * 2 + i % 2
            doc = doc_ref[jnp.maximum(block, 0)]
            mask = jnp.zeros((1, HD), jnp.float32)
            for q in range(4):
                seen = (block < query_blocks[q]) | ((block == query_blocks[q]) & alike)
                seen = seen & (block >= 0) & (doc == docs[q])
                mask = jnp.where(lane == q, jnp.where(seen, 0.0, BIG), mask)
            tile = pl.ds(pl.multiple_of(at * HALF_KEYS + i * HALF, HALF), HALF)
            kaug[tile, HD:] = jnp.broadcast_to(mask, (HALF, HD)).astype(jnp.bfloat16)

    def outward(dx, t):
        xd, yd = turn(x, dx, NX), yh * 2 + t
        src = o_out.at[pl.ds(t * 2, 2), pl.ds(pl.multiple_of(xd * 16, 16), 16), :]
        dst = out_ref.at[:, :, pl.ds(pl.multiple_of(my_head * COLS, COLS), COLS)]
        sem = out_recv.at[dx * 2 + ys]
        local = pltpu.make_async_copy(src, dst, sem)
        remote = pltpu.make_async_remote_copy(
            src_ref=src, dst_ref=dst, send_sem=out_send.at[dx * 2 + t], recv_sem=sem,
            device_id=device(xd, yd, z, c), device_id_type=MESH,
        )
        return local, remote

    def send_out(t):
        for dx in (2, 1, 3, 0):
            local, remote = outward(dx, t)
            if dx:
                remote.start()
            else:
                pl.when(ys == t)(local.start)
                pl.when(ys != t)(remote.start)

    def send_far():
        pl.when(zhi == 0)(lambda: pl.semaphore_wait(ack, 1))
        for which in range(2):
            hop(which, 0, 4).start()

    def set_out():
        @pl.when((zhi == 0) & ((lo < 4) | goes_up))
        def _():
            pl.semaphore_wait(ack, 1)
            for which in range(2):
                pl.when(lo < 4)(lambda: hop(which, 0, 4).start())
                pl.when(goes_up)(lambda: rest(which, 0).start())

    def pass_on():
        @pl.when(rests)
        def _():
            for which in range(2):
                rest(which, 0).wait_recv()
                rest(which, 1).start()

    def turn_up():
        @pl.when(lo == 6)
        def _():
            for which in range(2):
                landed(which, 9, 0)
                hop(which, 9, 5).start()

    ready(jnp.int32(0), 2)
    ready(jnp.int32(1), 2)

    def half_unit(u, _):
        i, h = lax.div(u, 2), lax.rem(u, 2)
        pl.when(u == 0)(set_out)
        pl.when(u == TRANSIT_AT)(pass_on)
        pl.when(u == TURN_AT)(turn_up)
        far_at = jnp.where(lo == 4, FAR_AT[4], jnp.where(lo == 5, FAR_AT[5], -1))
        pl.when(u == far_at)(send_far)
        pl.when(i < 7)(lambda: forward(h, i + 2 + (i > 2).astype(jnp.int32)))
        pl.when((u == 5) | (u == 6))(lambda: forward(1 - h, jnp.int32(5)))
        pl.when(i < UNITS - 1)(lambda: cross(h, i))

        @pl.when((h == 0) & (i > 0))
        def _():
            ready(crossed(i - 1), 3)
            ready(i + 1, 2)

        first = jnp.where(i == 0, 0, crossed(i - 1))
        second = i + 1

        @pl.when(valid(first) | valid(second))
        def _():
            @pl.when(h == 0)
            def _():
                def side_by_side(at):
                    near = (at == 1) | (i == 0)
                    prepare(jnp.where(at == 0, first, second), jnp.where(near, yh, 1 - yh), at)

                each(0, 2, side_by_side)

            def scores_of(q):
                return lax.dot_general(
                    qaug[q], kaug[...], (((1,), (1,)), ((), ())), preferred_element_type=jnp.float32
                )

            def soften(q, scores):
                before = top[q]
                after = jnp.maximum(before, jnp.max(scores, axis=1, keepdims=True))
                top[q] = after
                weights = jnp.exp2((scores - jnp.concatenate([after] * (KEYS // HD), axis=1)) * SCALE)
                return weights.astype(jnp.bfloat16), jnp.exp2((before - after) * SCALE)

            def mix(q, weights, factor):
                mixed = jnp.dot(weights, vaug[...], preferred_element_type=jnp.float32)
                acc[q] = acc[q] * jnp.concatenate([factor] * 2, axis=1) + mixed

            q = h * 2
            scores = scores_of(q)
            later_scores = scores_of(q + 1)
            weights, factor = soften(q, scores)
            later = soften(q + 1, later_scores)
            mix(q, weights, factor)
            mix(q + 1, *later)

        @pl.when(i == UNITS - 1)
        def _():
            def finish(j):
                q = h * 2 + j
                done = (acc[q, :, :HD] / acc[q, :, HD:]).astype(jnp.bfloat16)
                for g in range(GROUP):
                    o_out[q, :, pl.ds(g * HD, HD)] = done[g * HALF : (g + 1) * HALF]

            each(0, 2, finish)
            send_out(h)

        return 0

    lax.fori_loop(0, 2 * UNITS, half_unit, 0)

    def sent(i):
        for which in range(3):
            inward(which, i)[1].wait_send()

    each(1, 2 * NX, sent)

    def sent_on(p):
        @pl.when(valid(p))
        def _():
            for which in range(2):
                sends(which, p, lambda copy: copy.wait_send())

    each(0, SLICES, sent_on)

    def sent_across(m):
        p = crossed(m)

        @pl.when(valid(p))
        def _():
            for which in range(2):
                hop(which, p, 3).wait_send()

    each(0, UNITS - 1, sent_across)
    for which in range(2):
        pl.when(lo < 6)(lambda: hop(which, 0, 4).wait_send())
        pl.when(goes_up)(lambda: rest(which, 0).wait_send())
        pl.when(rests)(lambda: rest(which, 1).wait_send())
        pl.when(lo == 6)(lambda: hop(which, 9, 5).wait_send())
    for t in range(2):
        for dx in range(NX):
            local, remote = outward(dx, t)
            if dx:
                remote.wait_send()
            else:
                pl.when(ys != t)(remote.wait_send)
    for dx in range(NX):
        for s in range(2):
            pltpu.make_async_copy(
                o_out.at[pl.ds(0, 2), pl.ds(0, 16), :],
                out_ref.at[:, :, pl.ds(0, COLS)],
                out_recv.at[dx * 2 + s],
            ).wait()


def on_device(queries, keys, values, doc_ids):
    bf16, f32 = jnp.bfloat16, jnp.float32
    anywhere = pl.BlockSpec(memory_space=pl.ANY)
    return pl.pallas_call(
        kernel,
        out_shape=jax.ShapeDtypeStruct(queries.shape, bf16),
        in_specs=[pl.BlockSpec(memory_space=pltpu.SMEM)] + [pl.BlockSpec(memory_space=pltpu.HBM)] * 3,
        out_specs=anywhere,
        scratch_shapes=[
            pltpu.VMEM((2, SLICES, 4, 4, HALF, HD), bf16),
            pltpu.VMEM((2, 4, HALF, HD), bf16),
            pltpu.VMEM((4, HALF, COLS), bf16),
            pltpu.VMEM((4, ROWS, 2 * HD), bf16),
            pltpu.VMEM((KEYS, 2 * HD), bf16),
            pltpu.VMEM((KEYS, 2 * HD), bf16),
            pltpu.VMEM((4, ROWS, 2 * HD), f32),
            pltpu.VMEM((4, ROWS, HD), f32),
            pltpu.VMEM((4, HALF, COLS), bf16),
            pltpu.SemaphoreType.DMA((3, 8)),
            pltpu.SemaphoreType.DMA((3, 8)),
            pltpu.SemaphoreType.DMA((2, SLICES, 6)),
            pltpu.SemaphoreType.DMA((2, SLICES, 4)),
            pltpu.SemaphoreType.DMA((2, 2)),
            pltpu.SemaphoreType.DMA((2,)),
            pltpu.SemaphoreType.DMA((8,)),
            pltpu.SemaphoreType.DMA((8,)),
            pltpu.SemaphoreType.REGULAR,
        ],
        compiler_params=pltpu.CompilerParams(
            collective_id=0, has_side_effects=True, vmem_limit_bytes=62 * 1024 * 1024
        ),
        cost_estimate=pl.CostEstimate(
            flops=4 * ROWS * 4 * KEYS * UNITS * HD, bytes_accessed=2 * queries.size * 2, transcendentals=0
        ),
    )(doc_ids, queries, keys, values)


def solution(mesh):
    in_specs = (P("ctx", "head", None), P("ctx", "head", None), P("ctx", "head", None), P())
    out_specs = P("ctx", "head", None)
    return jax.shard_map(
        on_device, mesh=mesh, in_specs=in_specs, out_specs=out_specs, check_vma=False
    )
```

```python
import jax
import jax.numpy as jnp
from jax import lax
from jax.experimental import pallas as pl
from jax.experimental.pallas import tpu as pltpu
from jax.sharding import PartitionSpec as P

HD = 128
GROUP = 8
BLK = 128
HALF = 64
COLS = GROUP * HD
NX, NZ, NLO = 4, 16, 8

SLICES = 10
UNITS = 9
HALF_KEYS = 8 * HALF
KEYS = 2 * HALF_KEYS
ROWS = GROUP * HALF
BIG = -1e30
SCALE = HD**-0.5 * 1.4426950408889634
MESH = pl.DeviceIdType.MESH
FAR_AT = {4: 1, 5: 2}
TRANSIT_AT, TURN_AT = 5, 8


def back_of(p):
    return jnp.minimum(jnp.minimum(p, 4), SLICES - 1 - p)


def onward_of(p):
    return p + 1 + ((p == 3) | (p == 4)).astype(jnp.int32)


def kernel(
    doc_ref, q_ref, k_ref, v_ref, out_ref,
    kv, transit, q_in, qaug, kaug, vaug, acc, top, o_out,
    in_send, in_recv, hop_send, hop_recv, transit_send, transit_recv, out_send, out_recv, ack,
):
    head, ctx = lax.axis_index("head"), lax.axis_index("ctx")
    x, zhi = lax.rem(head, NX), lax.div(head, NX)
    lo, y, c = lax.div(ctx, 8), lax.rem(lax.div(ctx, 2), 4), lax.rem(ctx, 2)
    z = zhi * NLO + lo
    yh, ys = lax.div(y, 2), lax.rem(y, 2)

    def device(x, y, z, c):
        return (lax.div(z, NLO) * NX + x, lax.rem(z, NLO) * 8 + y * 2 + c)

    def turn(v, by, n):
        return lax.rem(v + by + n, n)

    def side(y):
        return lax.rem(lax.div(y + 1, 2), 2)

    y_pair = yh * 2 + 1 - ys
    y_same = 3 - y
    own, other = yh * 2 + c, (1 - yh) * 2 + c
    my_head = 2 * x + side(y)
    sibling = device(x, y, z, 1 - c)
    across = device(x, y_same, z, c)
    above = device(x, y, turn(z, 1, NZ), c)
    below = device(x, y, turn(z, -1, NZ), c)
    far_lo = jnp.minimum(lo + 4, NLO - 1)
    far = device(x, y, (1 - zhi) * NLO + far_lo, c)
    stop = device(x, y, (1 - zhi) * NLO + lax.rem(lo + 4, NLO), c)
    past_stop = device(x, y, zhi * NLO + lax.rem(lo + 4, NLO), c)
    rests, goes_up = (lo == 2) | (lo == 3), lo >= 6
    far_slot = jnp.where(lo < 4, 4, lo + 2)
    partners = [(dx, dy) for dx in range(NX) for dy in range(2)]
    to_above, to_below = lo < NLO - 1, lo > 0

    barrier = pltpu.get_barrier_semaphore()

    def greet(one):
        pl.semaphore_signal(barrier, inc=1, device_id=one, device_id_type=MESH)

    for dx, dy in partners[1:]:
        greet(device(turn(x, dx, NX), (y, y_pair)[dy], z, c))
    greet(sibling)
    greet(across)
    pl.when(to_above)(lambda: greet(above))
    pl.when(to_below)(lambda: greet(below))
    pl.when(goes_up)(lambda: greet(past_stop))

    def from_other_half(tell):
        for source in range(6):
            pl.when(lo == min(source + 4, NLO - 1))(lambda: tell(device(x, y, (1 - zhi) * NLO + source, c)))
        pl.when(rests)(lambda: tell(stop))

    pl.when(zhi == 0)(lambda: from_other_half(greet))
    pl.when((zhi == 0) & (lo < 6))(lambda: greet(far))
    pl.when((zhi == 0) & goes_up)(lambda: greet(stop))
    welcomed = jnp.where(lo == NLO - 1, 3, jnp.where(lo >= 2, 1, 0))
    count = to_above.astype(jnp.int32) + to_below.astype(jnp.int32) + rests.astype(jnp.int32)
    pl.semaphore_wait(barrier, 9 + zhi * (1 + welcomed) + count)

    def welcome(one):
        pl.semaphore_signal(ack, inc=1, device_id=one, device_id_type=MESH)

    pl.when(zhi == 1)(lambda: from_other_half(welcome))

    here = pl.ds(pl.multiple_of(x * 16, 16), 16)

    def inward(which, i):
        xd, yd = turn(x, lax.div(i, 2), NX), jnp.where(lax.rem(i, 2) == 0, y, y_pair)
        h = 2 * xd + side(yd)
        if which == 2:
            src = q_ref.at[:, :, pl.ds(pl.multiple_of(h * COLS, COLS), COLS)]
            dst = q_in.at[pl.ds(ys * 2, 2), here, :]
        else:
            src = (k_ref, v_ref)[which].at[:, :, pl.ds(pl.multiple_of(h * HD, HD), HD)]
            dst = kv.at[which, 0, own, pl.ds(ys * 2, 2), here, :]
        local = pltpu.make_async_copy(src, dst, in_recv.at[which, 0])
        remote = pltpu.make_async_remote_copy(
            src_ref=src, dst_ref=dst, send_sem=in_send.at[which, i], recv_sem=in_recv.at[which, i],
            device_id=device(xd, yd, z, c), device_id_type=MESH,
        )
        return local, remote

    def each(first, last, act):
        def step(i, _):
            act(i)
            return 0

        lax.fori_loop(first, last, step, 0)

    def arrived(which):
        inward(which, jnp.int32(0))[0].wait()
        each(1, 2 * NX, lambda i: inward(which, i)[1].wait_recv())

    for which in range(3):
        each(0, 2 * NX - 1, lambda k: inward(which, lax.rem(k + 3, 2 * NX - 1) + 1)[1].start())
        inward(which, jnp.int32(0))[0].start()

    def valid(p):
        return lo >= back_of(p)

    def hop(which, p, way):
        src, dst_p, slot = own, p, 0
        if way == 0:
            dst_p, to = onward_of(p), device(x, y, turn(z, jnp.where(p < 4, 1, -1), NZ), c)
        elif way == 1:
            to, slot = across, 1
        elif way == 2:
            to, slot = sibling, 2
        elif way == 3:
            src, to, slot = other, sibling, 3
        elif way == 4:
            dst_p, to = far_slot, far
        else:
            dst_p, to = 8, above
        return pltpu.make_async_remote_copy(
            src_ref=kv.at[which, p, src], dst_ref=kv.at[which, dst_p, src],
            send_sem=hop_send.at[which, p, way], recv_sem=hop_recv.at[which, dst_p, slot],
            device_id=to, device_id_type=MESH,
        )

    def rest(which, leg):
        return pltpu.make_async_remote_copy(
            src_ref=transit.at[which] if leg else kv.at[which, 0, own],
            dst_ref=kv.at[which, 9, own] if leg else transit.at[which],
            send_sem=transit_send.at[which, leg],
            recv_sem=hop_recv.at[which, 9, 0] if leg else transit_recv.at[which],
            device_id=past_stop if leg else stop, device_id_type=MESH,
        )

    def landed(which, p, slot):
        pltpu.make_async_remote_copy(
            src_ref=kv.at[which, p, own], dst_ref=kv.at[which, p, own],
            send_sem=hop_send.at[which, p, 1], recv_sem=hop_recv.at[which, p, slot],
            device_id=across, device_id_type=MESH,
        ).wait_recv()

    def sends(which, p, act):
        up, down = (p < 4) & to_above, (p == 4) | (p == 6) | (p == 7) | ((p == 8) & (lo < NLO - 1))
        pl.when(up | down)(lambda: act(hop(which, p, 0)))
        to_upper, to_lower = (p != 4) & (p != 5), (p != 0) & (p != 9)
        pl.when(((yh == 0) & to_upper) | ((yh == 1) & to_lower))(lambda: act(hop(which, p, 1)))
        act(hop(which, p, 2))

    def forward(which, p):
        @pl.when(valid(p))
        def _():
            pl.when((p != 9) | (lo != 6))(lambda: landed(which, p, 0))
            sends(which, p, lambda copy: copy.start())

    def crossed(m):
        return jnp.where(yh == 0, m + 1, jnp.where(m < 4, m, m + 2))

    def cross(which, m):
        p = crossed(m)

        @pl.when(valid(p))
        def _():
            landed(which, p, 1)
            hop(which, p, 3).start()

    def ready(p, slot):
        @pl.when(valid(p))
        def _():
            for which in range(2):
                landed(which, p, slot)

    lane = lax.broadcasted_iota(jnp.int32, (1, HD), 1)
    lanes = lax.broadcasted_iota(jnp.int32, (ROWS, HD), 1)
    ones = jnp.ones((HALF, HD), jnp.bfloat16)

    def mark(q):
        qaug[q, :, HD:] = jnp.where(lanes == q, 1.0, 0.0).astype(jnp.bfloat16)

    each(0, 4, mark)

    def fill(i):
        vaug[pl.ds(pl.multiple_of(i * HALF, HALF), HALF), HD:] = ones

    each(0, KEYS // HALF, fill)

    for which in range(2):
        arrived(which)
        sends(which, jnp.int32(0), lambda copy: copy.start())
        pl.when((zhi == 1) & (lo < 4))(lambda: hop(which, 0, 4).start())
        pl.when((zhi == 1) & goes_up)(lambda: rest(which, 0).start())
    each(0, 2, lambda which: forward(which, jnp.int32(1)))
    arrived(2)

    def begin(q):
        for g in range(GROUP):
            qaug[q, pl.ds(g * HALF, HALF), :HD] = q_in[q, :, pl.ds(g * HD, HD)]
        block_values = jnp.concatenate([kv[1, 0, own, q], ones], axis=1)
        scores = lax.dot_general(
            qaug[q, :, :HD], kv[0, 0, own, q], (((1,), (1,)), ((), ())), preferred_element_type=jnp.float32
        )
        key = lax.broadcasted_iota(jnp.int32, (ROWS, HALF), 1)
        token = lax.rem(lax.broadcasted_iota(jnp.int32, (ROWS, HALF), 0), HALF)
        scores = jnp.where(key <= token, scores, BIG)
        best = jnp.max(scores, axis=1, keepdims=True)
        weights = jnp.exp2((scores - best) * SCALE)
        acc[q] = jnp.dot(weights.astype(jnp.bfloat16), block_values, preferred_element_type=jnp.float32)
        top[q] = jnp.broadcast_to(best, (ROWS, HD))

    each(0, 4, begin)

    query_blocks = [lo * 16 + (yh * 2 + q // 2) * 4 + c * 2 + q % 2 for q in range(4)]

    def prepare(p, half_of_y, at):
        there = valid(p)
        rows = pl.ds(pl.multiple_of(at * HALF_KEYS, HALF_KEYS), HALF_KEYS)

        @pl.when(there)
        def _():
            kaug[rows, :HD] = kv[0, p, pl.ds(half_of_y * 2, 2)].reshape(HALF_KEYS, HD)
            vaug[rows, :HD] = kv[1, p, pl.ds(half_of_y * 2, 2)].reshape(HALF_KEYS, HD)

        @pl.when(jnp.logical_not(there))
        def _():
            kaug[rows, :HD] = jnp.zeros((HALF_KEYS, HD), jnp.bfloat16)
            vaug[rows, :HD] = jnp.zeros((HALF_KEYS, HD), jnp.bfloat16)

        back = back_of(p)
        alike = (p != 0) & (zhi == 1)
        docs = [doc_ref[b] for b in query_blocks]
        for i in range(8):
            block = (lo - back) * 16 + (half_of_y * 2 + i // 2 % 2) * 4 + i // 4 * 2 + i % 2
            doc = doc_ref[jnp.maximum(block, 0)]
            mask = jnp.zeros((1, HD), jnp.float32)
            for q in range(4):
                seen = (block < query_blocks[q]) | ((block == query_blocks[q]) & alike)
                seen = seen & (block >= 0) & (doc == docs[q])
                mask = jnp.where(lane == q, jnp.where(seen, 0.0, BIG), mask)
            tile = pl.ds(pl.multiple_of(at * HALF_KEYS + i * HALF, HALF), HALF)
            kaug[tile, HD:] = jnp.broadcast_to(mask, (HALF, HD)).astype(jnp.bfloat16)

    def outward(dx, t):
        xd, yd = turn(x, dx, NX), yh * 2 + t
        src = o_out.at[pl.ds(t * 2, 2), pl.ds(pl.multiple_of(xd * 16, 16), 16), :]
        dst = out_ref.at[:, :, pl.ds(pl.multiple_of(my_head * COLS, COLS), COLS)]
        sem = out_recv.at[dx * 2 + ys]
        local = pltpu.make_async_copy(src, dst, sem)
        remote = pltpu.make_async_remote_copy(
            src_ref=src, dst_ref=dst, send_sem=out_send.at[dx * 2 + t], recv_sem=sem,
            device_id=device(xd, yd, z, c), device_id_type=MESH,
        )
        return local, remote

    def send_out(t):
        for dx in (2, 1, 3, 0):
            local, remote = outward(dx, t)
            if dx:
                remote.start()
            else:
                pl.when(ys == t)(local.start)
                pl.when(ys != t)(remote.start)

    def send_far():
        pl.when(zhi == 0)(lambda: pl.semaphore_wait(ack, 1))
        for which in range(2):
            hop(which, 0, 4).start()

    def set_out():
        @pl.when((zhi == 0) & ((lo < 4) | goes_up))
        def _():
            pl.semaphore_wait(ack, 1)
            for which in range(2):
                pl.when(lo < 4)(lambda: hop(which, 0, 4).start())
                pl.when(goes_up)(lambda: rest(which, 0).start())

    def pass_on():
        @pl.when(rests)
        def _():
            for which in range(2):
                rest(which, 0).wait_recv()
                rest(which, 1).start()

    def turn_up():
        @pl.when(lo == 6)
        def _():
            for which in range(2):
                landed(which, 9, 0)
                hop(which, 9, 5).start()

    ready(jnp.int32(0), 2)
    ready(jnp.int32(1), 2)

    def half_unit(u, _):
        i, h = lax.div(u, 2), lax.rem(u, 2)
        pl.when(u == 0)(set_out)
        pl.when(u == TRANSIT_AT)(pass_on)
        pl.when(u == TURN_AT)(turn_up)
        far_at = jnp.where(lo == 4, FAR_AT[4], jnp.where(lo == 5, FAR_AT[5], -1))
        pl.when(u == far_at)(send_far)
        pl.when(i < 7)(lambda: forward(h, i + 2 + (i > 2).astype(jnp.int32)))
        pl.when((u == 5) | (u == 6))(lambda: forward(1 - h, jnp.int32(5)))
        pl.when(i < UNITS - 1)(lambda: cross(h, i))

        @pl.when((h == 0) & (i > 0))
        def _():
            ready(crossed(i - 1), 3)
            ready(i + 1, 2)

        first = jnp.where(i == 0, 0, crossed(i - 1))
        second = i + 1

        @pl.when(valid(first) | valid(second))
        def _():
            @pl.when(h == 0)
            def _():
                def side_by_side(at):
                    near = (at == 1) | (i == 0)
                    prepare(jnp.where(at == 0, first, second), jnp.where(near, yh, 1 - yh), at)

                each(0, 2, side_by_side)

            def scores_of(q):
                return lax.dot_general(
                    qaug[q], kaug[...], (((1,), (1,)), ((), ())), preferred_element_type=jnp.float32
                )

            def soften(q, scores):
                before = top[q]
                after = jnp.maximum(before, jnp.max(scores, axis=1, keepdims=True))
                top[q] = after
                weights = jnp.exp2((scores - jnp.concatenate([after] * (KEYS // HD), axis=1)) * SCALE)
                return weights.astype(jnp.bfloat16), jnp.exp2((before - after) * SCALE)

            def mix(q, weights, factor):
                mixed = jnp.dot(weights, vaug[...], preferred_element_type=jnp.float32)
                acc[q] = acc[q] * jnp.concatenate([factor] * 2, axis=1) + mixed

            q = h * 2
            scores = scores_of(q)
            later_scores = scores_of(q + 1)
            weights, factor = soften(q, scores)
            later = soften(q + 1, later_scores)
            mix(q, weights, factor)
            mix(q + 1, *later)

        @pl.when(i == UNITS - 1)
        def _():
            def finish(j):
                q = h * 2 + j
                done = (acc[q, :, :HD] / acc[q, :, HD:]).astype(jnp.bfloat16)
                for g in range(GROUP):
                    o_out[q, :, pl.ds(g * HD, HD)] = done[g * HALF : (g + 1) * HALF]

            each(0, 2, finish)
            send_out(h)

        return 0

    lax.fori_loop(0, 2 * UNITS, half_unit, 0)

    def sent(i):
        for which in range(3):
            inward(which, i)[1].wait_send()

    each(1, 2 * NX, sent)

    def sent_on(p):
        @pl.when(valid(p))
        def _():
            for which in range(2):
                sends(which, p, lambda copy: copy.wait_send())

    each(0, SLICES, sent_on)

    def sent_across(m):
        p = crossed(m)

        @pl.when(valid(p))
        def _():
            for which in range(2):
                hop(which, p, 3).wait_send()

    each(0, UNITS - 1, sent_across)
    for which in range(2):
        pl.when(lo < 6)(lambda: hop(which, 0, 4).wait_send())
        pl.when(goes_up)(lambda: rest(which, 0).wait_send())
        pl.when(rests)(lambda: rest(which, 1).wait_send())
        pl.when(lo == 6)(lambda: hop(which, 9, 5).wait_send())
    for t in range(2):
        for dx in range(NX):
            local, remote = outward(dx, t)
            if dx:
                remote.wait_send()
            else:
                pl.when(ys != t)(remote.wait_send)
    for dx in range(NX):
        for s in range(2):
            pltpu.make_async_copy(
                o_out.at[pl.ds(0, 2), pl.ds(0, 16), :],
                out_ref.at[:, :, pl.ds(0, COLS)],
                out_recv.at[dx * 2 + s],
            ).wait()


def on_device(queries, keys, values, doc_ids):
    bf16, f32 = jnp.bfloat16, jnp.float32
    anywhere = pl.BlockSpec(memory_space=pl.ANY)
    return pl.pallas_call(
        kernel,
        out_shape=jax.ShapeDtypeStruct(queries.shape, bf16),
        in_specs=[pl.BlockSpec(memory_space=pltpu.SMEM)] + [pl.BlockSpec(memory_space=pltpu.HBM)] * 3,
        out_specs=anywhere,
        scratch_shapes=[
            pltpu.VMEM((2, SLICES, 4, 4, HALF, HD), bf16),
            pltpu.VMEM((2, 4, HALF, HD), bf16),
            pltpu.VMEM((4, HALF, COLS), bf16),
            pltpu.VMEM((4, ROWS, 2 * HD), bf16),
            pltpu.VMEM((KEYS, 2 * HD), bf16),
            pltpu.VMEM((KEYS, 2 * HD), bf16),
            pltpu.VMEM((4, ROWS, 2 * HD), f32),
            pltpu.VMEM((4, ROWS, HD), f32),
            pltpu.VMEM((4, HALF, COLS), bf16),
            pltpu.SemaphoreType.DMA((3, 8)),
            pltpu.SemaphoreType.DMA((3, 8)),
            pltpu.SemaphoreType.DMA((2, SLICES, 6)),
            pltpu.SemaphoreType.DMA((2, SLICES, 4)),
            pltpu.SemaphoreType.DMA((2, 2)),
            pltpu.SemaphoreType.DMA((2,)),
            pltpu.SemaphoreType.DMA((8,)),
            pltpu.SemaphoreType.DMA((8,)),
            pltpu.SemaphoreType.REGULAR,
        ],
        compiler_params=pltpu.CompilerParams(
            collective_id=0, has_side_effects=True, vmem_limit_bytes=62 * 1024 * 1024
        ),
        cost_estimate=pl.CostEstimate(
            flops=4 * ROWS * 4 * KEYS * UNITS * HD, bytes_accessed=2 * queries.size * 2, transcendentals=0
        ),
    )(doc_ids, queries, keys, values)


def solution(mesh):
    in_specs = (P("ctx", "head", None), P("ctx", "head", None), P("ctx", "head", None), P())
    out_specs = P("ctx", "head", None)
    return jax.shard_map(
        on_device, mesh=mesh, in_specs=in_specs, out_specs=out_specs, check_vma=False
    )
```
